128 devices in a mesh: row: 8 (over y, x_lo), col: 16 (over x_hi, z, core).
Axes of the slice: x: 4 (x_hi: 2, x_lo: 2; x = x_hi * 2 + x_lo), y: 4, z: 4, core: 2. Of those that a mesh axis runs over, the one named last changes fastest.
Arguments:
- pair_rep: bfloat16 [1536, 1536, 128], P('row', 'col'), may hold values from -6 to 6
- res_mask: int32 [1536], replicated, may hold values 0 or 1
- norm_gain: float32 [128], replicated, may hold values from 0.1 to 1.9
- norm_bias: float32 [128], replicated, may hold values from -3 to 3
- w_left: bfloat16 [128, 128], replicated, may hold values from -0.5 to 0.5
- w_left_gate: bfloat16 [128, 128], replicated, may hold values from -0.5 to 0.5
- w_right: bfloat16 [128, 128], replicated, may hold values from -0.5 to 0.5
- w_right_gate: bfloat16 [128, 128], replicated, may hold values from -0.5 to 0.5
- w_out_gate: bfloat16 [128, 128], replicated, may hold values from -0.5 to 0.5
- out_gain: float32 [128], replicated, may hold values from 0.1 to 1.9
- out_bias: float32 [128], replicated, may hold values from -3 to 3
- w_out: bfloat16 [128, 128], replicated, may hold values from -0.5 to 0.5
Outputs:
- update_t: bfloat16 [1536, 1536, 128], P('col', 'row')
The draws below stay inside these ranges and needn't reach their ends.
All inputs are finite; a program needn't handle non-finite values.
Results may differ from the reference program's by a relative error of at most 0.0059.
Values may be sent and summed in bfloat16 or wider, within the bound.
A program may use at most 128 MiB of HBM per device.

```python
import jax
import jax.numpy as jnp
from jax import lax

CZ = 128
CH = 128
RES_BLK = 96
NRES = 1536
N_COL = 16


def with_ends(drawn, key, smallest, largest):
    longest = drawn.shape.index(max(drawn.shape))
    spots = []
    for shift in (0, 1):
        where = [jax.random.randint(jax.random.fold_in(key, axis), (), 0, length) for axis, length in enumerate(drawn.shape)]
        where[longest] = (where[longest] + shift) % drawn.shape[longest]
        spots.append(tuple(where))
    return drawn.at[spots[0]].set(smallest).at[spots[1]].set(largest)


def block_scale(rng, shape, cuts, smallest, top_value):
    def one(dim, blocks):
        heights = jax.random.uniform(jax.random.fold_in(jax.random.fold_in(rng, 6), dim), (blocks,), jnp.float32, smallest / len(cuts), top_value / len(cuts))
        return jnp.repeat(jnp.exp(heights), shape[dim] // blocks).reshape((-1,) + (1,) * (len(shape) - dim - 1))

    loudness = one(*cuts[0])
    for cut in cuts[1:]:
        loudness = loudness * one(*cut)
    return loudness


def bell_draw(own_key, extent, deviation, bound, split=(), dtype=jnp.bfloat16):
    result = jax.random.normal(own_key, extent, jnp.float32) * deviation
    if len(split) > 0:
        result = block_scale(own_key, extent, split, -0.22, 0.18) * result
    return jnp.clip(result, min=-bound, max=bound).astype(dtype)


def setup_inputs(seed: int = 0) -> dict:
    key_of = jax.random.split(jax.random.key(seed), 13)
    pair_rep = bell_draw(key_of[0], (NRES, NRES, CZ), 1.0, 6.0, ((0, 8), (1, 16)))
    res_mask = with_ends((jax.random.randint(key_of[1], (NRES,), 0, 8) < 7).astype(jnp.int32), jax.random.fold_in(key_of[1], 1), 0, 1)
    norm_gain = jnp.clip(1.0 + 0.18 * jax.random.normal(key_of[2], (CZ,), jnp.float32), 0.1, 1.9)
    norm_bias = bell_draw(key_of[3], (CZ,), 0.5, 3.0, (), jnp.float32)
    w_left = bell_draw(key_of[4], (CZ, CH), CZ ** -0.5, 0.5)
    w_left_gate = bell_draw(key_of[5], (CZ, CH), CZ ** -0.5, 0.5)
    w_right = bell_draw(key_of[6], (CZ, CH), CZ ** -0.5, 0.5)
    w_right_gate = bell_draw(key_of[7], (CZ, CH), CZ ** -0.5, 0.5)
    w_out_gate = bell_draw(key_of[8], (CZ, CZ), CZ ** -0.5, 0.5)
    out_gain = jnp.clip(1.0 + 0.18 * jax.random.normal(key_of[9], (CH,), jnp.float32), 0.1, 1.9)
    out_bias = bell_draw(key_of[10], (CH,), 0.5, 3.0, (), jnp.float32)
    w_out = bell_draw(key_of[11], (CH, CZ), CH ** -0.5, 0.5)
    return dict(pair_rep=pair_rep, res_mask=res_mask, norm_gain=norm_gain, norm_bias=norm_bias, w_left=w_left, w_left_gate=w_left_gate, w_right=w_right, w_right_gate=w_right_gate, w_out_gate=w_out_gate, out_gain=out_gain, out_bias=out_bias, w_out=w_out)


EPS = 1e-05

def norm_last(values, gain, bias):
    mean = lax.optimization_barrier(jnp.mean(values, axis=-1, keepdims=True))
    centred = values - mean
    var = lax.optimization_barrier(jnp.mean(centred * centred, axis=-1, keepdims=True))
    return centred * lax.rsqrt(var + EPS) * gain + bias

def reference(pair_rep, res_mask, norm_gain, norm_bias, w_left, w_left_gate, w_right, w_right_gate, w_out_gate, out_gain, out_bias, w_out):
    mask_f = res_mask.astype(jnp.float32)
    starts = (jnp.arange(N_COL) * RES_BLK).astype(jnp.int32)

    def front(start):
        block = lax.dynamic_slice_in_dim(pair_rep, start, RES_BLK, 0)
        normed = norm_last(block.astype(jnp.float32), norm_gain, norm_bias).astype(jnp.bfloat16)
        pmask = lax.dynamic_slice_in_dim(mask_f, start, RES_BLK)[:, None] * mask_f[None, :]
        normed_f = normed.astype(jnp.float32)

        def project(w_value, w_gate):
            value = jnp.einsum('ikd,dc->cik', normed_f, w_value.astype(jnp.float32))
            gate = jnp.einsum('ikd,dc->cik', normed_f, w_gate.astype(jnp.float32))
            return (jax.nn.sigmoid(gate) * value * pmask[None]).astype(jnp.bfloat16)
        return (project(w_left, w_left_gate), project(w_right, w_right_gate))
    left, right = lax.map(front, starts)

    def triangle(channel):
        left_c = lax.dynamic_index_in_dim(left, channel, 1, keepdims=False).reshape(NRES, NRES)
        right_c = lax.dynamic_index_in_dim(right, channel, 1, keepdims=False).reshape(NRES, NRES)
        return jnp.dot(right_c, left_c.T, preferred_element_type=jnp.float32).astype(jnp.bfloat16)
    product = lax.map(triangle, jnp.arange(CH).astype(jnp.int32))

    def back(start):
        block = lax.dynamic_slice_in_dim(product, start, RES_BLK, 1).astype(jnp.float32)
        mean = lax.optimization_barrier(jnp.mean(block, axis=0, keepdims=True))
        centred = block - mean
        var = lax.optimization_barrier(jnp.mean(centred * centred, axis=0, keepdims=True))
        tnorm = (centred * lax.rsqrt(var + EPS) * out_gain[:, None, None] + out_bias[:, None, None]).astype(jnp.bfloat16)
        proj = jnp.einsum('cji,cd->jid', tnorm.astype(jnp.float32), w_out.astype(jnp.float32))
        column = lax.dynamic_slice_in_dim(pair_rep, start, RES_BLK, 1)
        normed = norm_last(column.astype(jnp.float32), norm_gain, norm_bias).astype(jnp.bfloat16)
        gate = jnp.einsum('ijc,cd->jid', normed.astype(jnp.float32), w_out_gate.astype(jnp.float32))
        return (jax.nn.sigmoid(gate) * proj).astype(jnp.bfloat16)
    return lax.map(back, starts).reshape(NRES, NRES, CZ)
```

```python
import jax
import jax.numpy as jnp
from jax import lax
from jax.experimental import pallas as pl
from jax.experimental.pallas import tpu as pltpu
from jax.sharding import PartitionSpec as P

EPS = 1e-05
N_ROW, N_COL = 8, 16
N_DEV = N_ROW * N_COL
NI, NK, CH = 192, 96, 128
PARTS = 3
KP = NK // PARTS
HP = KP // 2
TP = KP + HP
F32, BF16 = jnp.float32, jnp.bfloat16
MESH = pl.DeviceIdType.MESH


def coords():
    row, col = lax.axis_index("row"), lax.axis_index("col")
    return (col // 8) * 2 + row % 2, row // 2, (col // 2) % 4, col % 2


def each_peer(fn):
    x, y, z, core = coords()
    first = (x * 16 + y * 4 + z) * 5 + core * 64

    def body(s, _):
        t = (s + first) % N_DEV

        @pl.when(t != 0)
        def _():
            px, py, pz, pc = (x + t % 4) % 4, (y + t // 4 % 4) % 4, (z + t // 16 % 4) % 4, (core + t // 64) % 2
            fn(py * 2 + px % 2, (px // 2) * 8 + pz * 2 + pc)

        return 0

    lax.fori_loop(0, N_DEV, body, 0)


def send_part(src, dst, part, send_sem, recv_sem):
    me = lax.axis_index("row") * N_COL + lax.axis_index("col")

    def send(row, col):
        pltpu.make_async_remote_copy(
            src_ref=src.at[part, row * N_COL + col],
            dst_ref=dst.at[part, me],
            send_sem=send_sem.at[part],
            recv_sem=recv_sem.at[part],
            device_id={"row": row, "col": col},
            device_id_type=MESH,
        ).start()

    each_peer(send)
    dst[part, me] = src[part, me]


def wait_part(ref, part, sem):
    whole = ref.at[part, pl.ds(0, N_DEV - 1)]
    pltpu.make_async_copy(whole, whole, sem.at[part]).wait()


def loop(n, body, unroll=1):
    lax.fori_loop(0, n, lambda i, c: (body(i), c)[1], 0, unroll=unroll)


def low_lanes(shape):
    return lax.broadcasted_iota(jnp.int32, shape, 1) < 64


def kernel(
    z_hbm, mask_i, mask_s, gain, bias, w_l, w_lg, w_r, w_rg, w_og, og_s, ob_s, w_o,
    out_hbm,
    zb, nb, n32, s32, wt, send_r, send_l, recv_r, recv_l, right_t, left, recv_t, ob,
    z_sem, out_sem, rs, rr, ls, lr, ts, tr,
):
    row, col = lax.axis_index("row"), lax.axis_index("col")
    barrier = pltpu.get_barrier_semaphore()
    for p in range(PARTS):
        pltpu.make_async_copy(z_hbm.at[:, pl.ds(p * KP, KP), :], zb.at[p], z_sem.at[p]).start()
    each_peer(
        lambda r, c: pl.semaphore_signal(barrier, inc=1, device_id={"row": r, "col": c}, device_id_type=MESH)
    )

    wt[0] = w_r[...].T
    wt[1] = (w_rg[...].astype(F32) * 0.5).astype(BF16).T
    wt[2] = w_l[...].T
    wt[3] = (w_lg[...].astype(F32) * 0.5).astype(BF16).T

    def normalise(p):
        def body(i):
            v = zb[p, pl.ds(i * 4, 4)].astype(F32).reshape(4 * KP, CH)
            mean = jnp.mean(v, axis=-1, keepdims=True)
            c = v - mean
            var = jnp.mean(c * c, axis=-1, keepdims=True)
            n32[pl.ds(pl.multiple_of(i * 4 * KP, 4 * KP), 4 * KP), :] = (
                c * lax.rsqrt(var + EPS) * gain[...] + bias[...]
            )

        loop(NI // 4, body)

        def main(t):
            nb[p, t] = n32[pl.ds(t, 128, stride=KP), :].astype(BF16)

        loop(KP, main)

        def extra(t):
            nb[p, KP + t, 0:64] = n32[pl.ds(128 * KP + t, 64, stride=KP), :].astype(BF16)
            nb[p, KP + t, 64:128] = n32[pl.ds(128 * KP + HP + t, 64, stride=KP), :].astype(BF16)

        loop(HP, extra)

    def project(p, which, send):
        weights = wt[2 * which : 2 * which + 2].reshape(2 * CH, CH)
        k0 = col * NK + p * KP
        lanes = mask_i[pl.ds(row, 1), :] * 0.5

        def mask(k):
            return mask_s[k0 + k].astype(F32)

        def pair(t, mask_a, mask_b):
            rhs = nb[p, pl.ds(t, 2)].reshape(256, CH)
            both = lax.dot_general(weights, rhs, (((1,), (1,)), ((), ())), preferred_element_type=F32)
            gated = (jnp.tanh(both[CH:]) + 1.0) * both[:CH]
            s32[pl.ds(t, CH, stride=TP), :] = gated[:, :128] * mask_a
            s32[pl.ds(t + 1, CH, stride=TP), :] = gated[:, 128:] * mask_b

        def main(i):
            t = i * 2
            pair(t, lanes[:, :128] * mask(t), lanes[:, :128] * mask(t + 1))

        loop(KP // 2, main)

        def extra(i):
            t = i * 2
            pair(
                KP + t,
                lanes[:, 128:256] * mask(t) + lanes[:, 256:] * mask(t + HP),
                lanes[:, 128:256] * mask(t + 1) + lanes[:, 256:] * mask(t + 1 + HP),
            )

        loop(HP // 2, extra)

        def pack(i):
            rows = s32[pl.ds(pl.multiple_of(i * 4 * TP, 4 * TP), 4 * TP), :]
            send[p, pl.ds(i * 4, 4)] = rows.astype(BF16).reshape(4, TP, 128)

        loop(CH // 4, pack)

    def gate(p):
        def body(i):
            t = i * 2
            v = nb[p, pl.ds(t, 2)].reshape(256, CH)
            g = jnp.dot(v, w_og[...], preferred_element_type=F32)
            nb[p, pl.ds(t, 2)] = (0.5 * jnp.tanh(0.5 * g) + 0.5).astype(BF16).reshape(2, 128, CH)

        loop(TP // 2, body)

    def halves(ref, p, y, q):
        a = ref[p, pl.ds((2 * y) * N_COL + q, 4), KP:TP, :].astype(F32).reshape(4 * HP, 128)
        b = ref[p, pl.ds((2 * y + 1) * N_COL + q, 4), KP:TP, :].astype(F32).reshape(4 * HP, 128)
        low = low_lanes(a.shape)
        h0 = jnp.where(low, a, pltpu.roll(b, 64, 1)).reshape(4, 1, HP, 128)
        h1 = jnp.where(low, pltpu.roll(a, 64, 1), b).reshape(4, 1, HP, 128)
        return jnp.concatenate([h0, h1], axis=1).reshape(4 * KP, 128).astype(BF16)

    def take_right(p):
        def body(i):
            y, q = i // 4, i % 4 * 4
            lane = pl.ds(pl.multiple_of(p * N_COL * KP + q * KP, 128), 128)

            def put(r, first, tile, size):
                for l in range(0, size, KP):
                    at = first + l
                    dest = (at % NK) // KP * (N_COL * KP) + (2 * r + at // NK) * KP
                    right_t[pl.ds(pl.multiple_of(dest, KP), KP), lane] = tile[l : l + KP]

            for r in (2 * y, 2 * y + 1):
                put(r, 0, recv_r[p, pl.ds(r * N_COL + q, 4), 0:KP, :].reshape(128, 128).T, 128)
            both = halves(recv_r, p, y, q).T
            put(2 * y, 128, both[:64], 64)
            put(2 * y + 1, 128, both[64:], 64)

        loop(16, body)

    def take_left(p):
        def body(i):
            y, q = i // 4, i % 4 * 4
            k = pl.ds(pl.multiple_of(p * N_COL * KP + q * KP, 128), 128)
            for x in range(2):
                left[y, k, x * 128 : (x + 1) * 128] = recv_l[
                    p, pl.ds((2 * y + x) * N_COL + q, 4), 0:KP, :
                ].reshape(128, 128)
            left[y, k, 256:384] = halves(recv_l, p, y, q)

        loop(16, body)

    def product(s):
        def body(y):
            rows = right_t[pl.ds(s * N_COL * KP, N_COL * KP), :]
            tri = jnp.dot(rows, left[y], preferred_element_type=F32)
            for x in range(2):
                send_r[s, pl.ds((2 * y + x) * N_COL, N_COL), 0:KP, :] = (
                    tri[:, x * 128 : (x + 1) * 128].astype(BF16).reshape(N_COL, KP, 128)
                )
            last = tri[:, 256:].reshape(N_COL, 2, HP, 128)
            a, b = last[:, 0].reshape(N_COL * HP, 128), last[:, 1].reshape(N_COL * HP, 128)
            low = low_lanes(a.shape)
            e0 = jnp.where(low, a, pltpu.roll(b, 64, 1)).astype(BF16)
            e1 = jnp.where(low, pltpu.roll(a, 64, 1), b).astype(BF16)
            send_r[s, pl.ds((2 * y) * N_COL, N_COL), KP:TP, :] = e0.reshape(N_COL, HP, 128)
            send_r[s, pl.ds((2 * y + 1) * N_COL, N_COL), KP:TP, :] = e1.reshape(N_COL, HP, 128)

        loop(4, body)

    def finish(s):
        slot = s % 2
        step = 8

        def norm(g):
            rows = pl.ds(pl.multiple_of(g * 16, 16), 16)

            def some(i):
                return recv_t[s, pl.ds(i * step, step), rows, :].astype(F32)

            zero = jnp.zeros((16, 128), F32)
            mean = lax.fori_loop(0, CH // step, lambda i, a: a + jnp.sum(some(i), axis=0), zero) / CH

            def square(i, a):
                c = some(i) - mean[None]
                return a + jnp.sum(c * c, axis=0)

            var = lax.fori_loop(0, CH // step, square, zero) / CH
            scale = lax.rsqrt(var + EPS)

            def put(i):
                c = some(i) - mean[None]
                for e in range(step):
                    ch = i * step + e
                    s32[pl.ds(pl.multiple_of(ch * TP + g * 16, 16), 16), :] = c[e] * scale * og_s[ch] + ob_s[ch]

            loop(CH // step, put)

        loop(TP // 16, norm)

        def tile(t):
            v = s32[pl.ds(t, CH, stride=TP), :].astype(BF16)
            proj = jnp.dot(v.T, w_o[...], preferred_element_type=F32)
            return (proj * nb[s, t].astype(F32)).astype(BF16)

        def main(t):
            ob[slot, t, 0:128] = tile(t)

        loop(KP, main)

        def extra(t):
            v = tile(KP + t)
            ob[slot, t, 128:192] = v[:64]
            ob[slot, t + HP, 128:192] = v[64:]

        loop(HP, extra)
        return pltpu.make_async_copy(ob.at[slot], out_hbm.at[pl.ds(s * KP, KP)], out_sem.at[slot])

    for p in range(PARTS):
        pltpu.make_async_copy(z_hbm.at[:, pl.ds(p * KP, KP), :], zb.at[p], z_sem.at[p]).wait()
        normalise(p)
        project(p, 0, send_r)
        if p == 0:
            pl.semaphore_wait(barrier, N_DEV - 1)
        send_part(send_r, recv_r, p, rs, rr)
    for p in range(PARTS):
        project(p, 1, send_l)
        send_part(send_l, recv_l, p, ls, lr)
    for p in range(PARTS):
        gate(p)
    for p in range(PARTS):
        wait_part(recv_r, p, rr)
        take_right(p)
    for p in range(PARTS):
        wait_part(send_r, p, rs)
    for p in range(PARTS):
        wait_part(recv_l, p, lr)
        take_left(p)
    for s in range(PARTS):
        product(s)
        send_part(send_r, recv_t, s, ts, tr)
    stores = []
    for s in range(PARTS):
        wait_part(recv_t, s, tr)
        if s >= 2:
            stores[s - 2].wait()
        stores.append(finish(s))
        stores[s].start()
    for s in range(max(0, PARTS - 2), PARTS):
        stores[s].wait()
    for p in range(PARTS):
        wait_part(send_l, p, ls)
        wait_part(send_r, p, ts)


def on_device(
    pair_rep, res_mask, norm_gain, norm_bias, w_left, w_left_gate, w_right, w_right_gate, w_out_gate,
    out_gain, out_bias, w_out,
):
    by_row = res_mask.astype(F32).reshape(N_ROW, NI)
    none = jnp.zeros((N_ROW, 64), F32)
    mask_i = jnp.concatenate([by_row, none, none, by_row[:, 128:]], axis=1)
    vmem = pl.BlockSpec(memory_space=pltpu.VMEM)
    smem = pl.BlockSpec(memory_space=pltpu.SMEM)
    hbm = pl.BlockSpec(memory_space=pl.ANY)
    dma = pltpu.SemaphoreType.DMA
    slots = pltpu.VMEM((PARTS, N_DEV, TP, 128), BF16)
    return pl.pallas_call(
        kernel,
        out_shape=jax.ShapeDtypeStruct((NK, NI, CH), BF16),
        in_specs=[hbm, vmem, smem] + [vmem] * 7 + [smem, smem, vmem],
        out_specs=hbm,
        scratch_shapes=[
            pltpu.VMEM((PARTS, NI, KP, CH), BF16),
            pltpu.VMEM((PARTS, TP, 128, CH), BF16),
            pltpu.VMEM((NI * KP, CH), F32),
            pltpu.VMEM((CH * TP, 128), F32),
            pltpu.VMEM((4, CH, CH), BF16),
            slots, slots, slots, slots,
            pltpu.VMEM((N_COL * NK, N_COL * NK), BF16),
            pltpu.VMEM((4, N_COL * NK, 2 * NI), BF16),
            slots,
            pltpu.VMEM((2, KP, NI, CH), BF16),
            dma((PARTS,)), dma((2,)),
            dma((PARTS,)), dma((PARTS,)), dma((PARTS,)), dma((PARTS,)), dma((PARTS,)), dma((PARTS,)),
        ],
        compiler_params=pltpu.CompilerParams(
            collective_id=0, has_side_effects=True, vmem_limit_bytes=60 << 20
        ),
        cost_estimate=pl.CostEstimate(flops=11 * 10**9, bytes_accessed=10**7, transcendentals=7 * 10**6),
    )(
        pair_rep, mask_i, res_mask, norm_gain[None], norm_bias[None], w_left, w_left_gate, w_right,
        w_right_gate, w_out_gate, out_gain, out_bias, w_out,
    )


def solution(mesh):
    placed = (P("row", "col", None), P(), P(), P(), P(), P(), P(), P(), P(), P(), P(), P())
    return jax.shard_map(
        on_device, mesh=mesh, in_specs=placed, out_specs=P("col", "row", None), check_vma=False
    )
```

```python
import jax
import jax.numpy as jnp
from jax import lax
from jax.experimental import pallas as pl
from jax.experimental.pallas import tpu as pltpu
from jax.sharding import PartitionSpec as P

EPS = 1e-05
N_ROW, N_COL = 8, 16
N_DEV = N_ROW * N_COL
NI, NK, CH = 192, 96, 128
PARTS = 3
IP = NI // PARTS
TP = NK // 2
F32, BF16 = jnp.float32, jnp.bfloat16
MESH = pl.DeviceIdType.MESH


def coords():
    row, col = lax.axis_index("row"), lax.axis_index("col")
    return (col // 8) * 2 + row % 2, row // 2, (col // 2) % 4, col % 2


def each_peer(fn):
    x, y, z, core = coords()
    first = (x * 16 + y * 4 + z) * 5 + core * 64

    def body(s, _):
        t = (s + first) % N_DEV

        @pl.when(t != 0)
        def _():
            px, py, pz, pc = (x + t % 4) % 4, (y + t // 4 % 4) % 4, (z + t // 16 % 4) % 4, (core + t // 64) % 2
            fn(py * 2 + px % 2, (px // 2) * 8 + pz * 2 + pc)

        return 0

    lax.fori_loop(0, N_DEV, body, 0)


def send_part(src, dst, part, send_sem, recv_sem):
    me = lax.axis_index("row") * N_COL + lax.axis_index("col")

    def send(row, col):
        pltpu.make_async_remote_copy(
            src_ref=src.at[part, row * N_COL + col],
            dst_ref=dst.at[part, me],
            send_sem=send_sem.at[part],
            recv_sem=recv_sem.at[part],
            device_id={"row": row, "col": col},
            device_id_type=MESH,
        ).start()

    each_peer(send)
    dst[part, me] = src[part, me]


def wait_part(ref, part, sem):
    whole = ref.at[part, pl.ds(0, N_DEV - 1)]
    pltpu.make_async_copy(whole, whole, sem.at[part]).wait()


def loop(n, body, unroll=1):
    lax.fori_loop(0, n, lambda i, c: (body(i), c)[1], 0, unroll=unroll)


def low_lanes(shape):
    return lax.broadcasted_iota(jnp.int32, shape, len(shape) - 1) < 64


def swap_halves(a, b):
    low = low_lanes(a.shape)
    return jnp.where(low, a, pltpu.roll(b, 64, 1)), jnp.where(low, pltpu.roll(a, 64, 1), b)


def kernel(
    z_hbm, mask_v, mask_s, gain, bias, w_l, w_lg, w_r, w_rg, w_og, og_s, ob_s, w_o,
    out_hbm,
    zb, nb, n32, s32, wt, send_r, send_l, recv_r, recv_l, right_t, left, recv_t, ob,
    z_sem, out_sem, rs, rr, ls, lr, ts, tr,
):
    row, col = lax.axis_index("row"), lax.axis_index("col")
    barrier = pltpu.get_barrier_semaphore()

    def load(p):
        return pltpu.make_async_copy(z_hbm.at[pl.ds(p * IP, IP)], zb.at[p], z_sem.at[p])

    for p in range(PARTS):
        load(p).start()
    each_peer(
        lambda r, c: pl.semaphore_signal(barrier, inc=1, device_id={"row": r, "col": c}, device_id_type=MESH)
    )

    wt[0] = w_r[...].T
    wt[1] = (w_rg[...].astype(F32) * 0.5).astype(BF16).T
    wt[2] = w_l[...].T
    wt[3] = (w_lg[...].astype(F32) * 0.5).astype(BF16).T

    def normalise(p):
        ones = jnp.ones((2 * CH, CH), BF16)

        def body(i):
            v = zb[p, pl.ds(i * 2, 2)].reshape(2 * NK, CH)
            mean = jnp.dot(v, ones[:CH], preferred_element_type=F32) * (1 / CH)
            c = v.astype(F32) - mean
            sq = c * c
            high = sq.astype(BF16)
            rest = (sq - high.astype(F32)).astype(BF16)
            var = jnp.dot(jnp.concatenate([high, rest], axis=1), ones, preferred_element_type=F32) * (1 / CH)
            n32[pl.ds(pl.multiple_of(i * 2 * NK, 2 * NK), 2 * NK), :] = c * lax.rsqrt(var + EPS) * gain[...] + bias[...]

        loop(IP // 2, body, 2)

        def tile(t):
            nb[p, t, 0:64] = n32[pl.ds(t, 64, stride=NK), :].astype(BF16)
            nb[p, t, 64:128] = n32[pl.ds(TP + t, 64, stride=NK), :].astype(BF16)

        loop(TP, tile, 4)

    def project(p, which, send):
        weights = wt[2 * which : 2 * which + 2].reshape(2 * CH, CH)
        group = 3 * row + p
        low = low_lanes((1, 128))
        m = mask_v[pl.ds(group // 2, 1), :].astype(F32) * 0.5
        other = pltpu.roll(m, 64, 1)
        first = jnp.where(group % 2 == 0, m, other)
        second = jnp.where(group % 2 == 0, other, m)
        lanes = jnp.where(low, first, second)

        def mask(t):
            k = col * NK + t
            return lanes * jnp.where(low, mask_s[k].astype(F32), mask_s[k + TP].astype(F32))

        def pair(i):
            t = i * 2
            rhs = nb[p, pl.ds(t, 2)].reshape(256, CH)
            both = lax.dot_general(weights, rhs, (((1,), (1,)), ((), ())), preferred_element_type=F32)
            gated = (jnp.tanh(both[CH:]) + 1.0) * both[:CH]
            s32[pl.ds(t, CH, stride=TP), :] = gated[:, :128] * mask(t)
            s32[pl.ds(t + 1, CH, stride=TP), :] = gated[:, 128:] * mask(t + 1)

        loop(TP // 2, pair, 2)

        def pack(i):
            rows = s32[pl.ds(pl.multiple_of(i * 4 * TP, 4 * TP), 4 * TP), :]
            send[p, pl.ds(i * 4, 4)] = rows.astype(BF16).reshape(4, TP, 128)

        loop(CH // 4, pack, 2)

    def gate(p):
        def body(i):
            t = i * 2
            v = nb[p, pl.ds(t, 2)].reshape(256, CH)
            g = jnp.dot(v, w_og[...], preferred_element_type=F32)
            nb[p, pl.ds(t, 2)] = (0.5 * jnp.tanh(0.5 * g) + 0.5).astype(BF16).reshape(2, 128, CH)

        loop(TP // 2, body, 2)

    def two_rows(ref, p, y, q):
        a = ref[p, pl.ds((2 * y) * N_COL + q, 4)].astype(F32).reshape(4 * TP, 128)
        b = ref[p, pl.ds((2 * y + 1) * N_COL + q, 4)].astype(F32).reshape(4 * TP, 128)
        h0, h1 = swap_halves(a, b)
        both = jnp.concatenate([h0.reshape(4, 1, TP, 128), h1.reshape(4, 1, TP, 128)], axis=1)
        return both.reshape(4 * NK, 128).astype(BF16)

    def take_right(p):
        def body(i):
            y, q = i // 4, i % 4 * 4
            tile = two_rows(recv_r, p, y, q).T
            lane = pl.ds(pl.multiple_of(q * NK, 128), 4 * NK)
            for x in range(2):
                at = pl.multiple_of((2 * y + x) * NI + p * IP, IP)
                right_t[pl.ds(at, IP), lane] = tile[x * 64 : (x + 1) * 64]

        loop(16, body)

    def take_left(p):
        def body(i):
            y, q = i // 4, i % 4 * 4
            left[y, pl.ds(pl.multiple_of(q * NK, 128), 4 * NK), :] = two_rows(recv_l, p, y, q)

        loop(16, body)

    def product(s):
        def body(i):
            y, h = i // 4 * 2, i % 4
            rows = right_t[pl.ds(pl.multiple_of(h * 384, 384), 384), :]
            cols = jnp.concatenate([left[y], left[y + 1]], axis=1)
            tri = jnp.dot(rows, cols, preferred_element_type=F32)
            for x in range(2):
                both = tri[:, x * 128 : (x + 1) * 128].reshape(4, 2, TP, 128)
                e = swap_halves(both[:, 0].reshape(4 * TP, 128), both[:, 1].reshape(4 * TP, 128))
                for r in range(2):
                    slot = (2 * (y + x) + r) * N_COL + h * 4
                    send_r[s, pl.ds(slot, 4)] = e[r].astype(BF16).reshape(4, TP, 128)

        loop(8, body)

    def finish(s):
        slot = s % 2
        step = 16

        def norm(g):
            rows = pl.ds(pl.multiple_of(g * 16, 16), 16)

            def some(i):
                return recv_t[s, pl.ds(i * step, step), rows, :].astype(F32)

            zero = jnp.zeros((16, 128), F32)
            mean = lax.fori_loop(0, CH // step, lambda i, a: a + jnp.sum(some(i), axis=0), zero) * (1 / CH)

            def square(i, a):
                c = some(i) - mean[None]
                return a + jnp.sum(c * c, axis=0)

            var = lax.fori_loop(0, CH // step, square, zero) * (1 / CH)
            scale = lax.rsqrt(var + EPS)

            def put(i):
                c = some(i) - mean[None]
                for e in range(step):
                    ch = i * step + e
                    s32[pl.ds(pl.multiple_of(ch * TP + g * 16, 16), 16), :] = c[e] * scale * og_s[ch] + ob_s[ch]

            loop(CH // step, put)

        loop(TP // 16, norm)

        def tile(t):
            v = s32[pl.ds(t, CH, stride=TP), :].astype(BF16)
            proj = jnp.dot(v.T, w_o[...], preferred_element_type=F32)
            out = (proj * nb[s, t].astype(F32)).astype(BF16)
            ob[slot, t] = out[:64]
            ob[slot, t + TP] = out[64:]

        loop(TP, tile, 4)

    def store(s):
        return pltpu.make_async_copy(ob.at[s % 2], out_hbm.at[:, pl.ds(s * IP, IP)], out_sem.at[s % 2])

    for p in range(PARTS):
        load(p).wait()
        normalise(p)
        project(p, 0, send_r)
        if p == 0:
            pl.semaphore_wait(barrier, N_DEV - 1)
        send_part(send_r, recv_r, p, rs, rr)
    for p in range(PARTS):
        project(p, 1, send_l)
        send_part(send_l, recv_l, p, ls, lr)
    for p in range(PARTS):
        gate(p)
    for p in range(PARTS):
        wait_part(recv_r, p, rr)
        take_right(p)
    for p in range(PARTS):
        wait_part(send_r, p, rs)
        wait_part(recv_l, p, lr)
        take_left(p)
        product(p)
        send_part(send_r, recv_t, p, ts, tr)
    for p in range(PARTS):
        wait_part(recv_t, p, tr)
        if p >= 2:
            store(p - 2).wait()
        finish(p)
        store(p).start()
    for p in range(max(0, PARTS - 2), PARTS):
        store(p).wait()
    for p in range(PARTS):
        wait_part(send_l, p, ls)
        wait_part(send_r, p, ts)


def on_device(
    pair_rep, res_mask, norm_gain, norm_bias, w_left, w_left_gate, w_right, w_right_gate, w_out_gate,
    out_gain, out_bias, w_out,
):
    vmem = pl.BlockSpec(memory_space=pltpu.VMEM)
    smem = pl.BlockSpec(memory_space=pltpu.SMEM)
    hbm = pl.BlockSpec(memory_space=pl.ANY)
    dma = pltpu.SemaphoreType.DMA
    slots = pltpu.VMEM((PARTS, N_DEV, TP, 128), BF16)
    return pl.pallas_call(
        kernel,
        out_shape=jax.ShapeDtypeStruct((NK, NI, CH), BF16),
        in_specs=[hbm, vmem, smem] + [vmem] * 7 + [smem, smem, vmem],
        out_specs=hbm,
        scratch_shapes=[
            pltpu.VMEM((PARTS, IP, NK, CH), BF16),
            pltpu.VMEM((PARTS, TP, 128, CH), BF16),
            pltpu.VMEM((IP * NK, CH), F32),
            pltpu.VMEM((CH * TP, 128), F32),
            pltpu.VMEM((4, CH, CH), BF16),
            slots, slots, slots, slots,
            pltpu.VMEM((N_COL * NK, N_COL * NK), BF16),
            pltpu.VMEM((4, N_COL * NK, 128), BF16),
            slots,
            pltpu.VMEM((2, NK, IP, CH), BF16),
            dma((PARTS,)), dma((2,)),
            dma((PARTS,)), dma((PARTS,)), dma((PARTS,)), dma((PARTS,)), dma((PARTS,)), dma((PARTS,)),
        ],
        compiler_params=pltpu.CompilerParams(
            collective_id=0, has_side_effects=True, vmem_limit_bytes=60 << 20
        ),
        cost_estimate=pl.CostEstimate(flops=11 * 10**9, bytes_accessed=10**7, transcendentals=7 * 10**6),
    )(
        pair_rep, res_mask.reshape(12, 128), res_mask, norm_gain[None], norm_bias[None], w_left, w_left_gate, w_right,
        w_right_gate, w_out_gate, out_gain, out_bias, w_out,
    )


def solution(mesh):
    placed = (P("row", "col", None), P(), P(), P(), P(), P(), P(), P(), P(), P(), P(), P())
    return jax.shard_map(
        on_device, mesh=mesh, in_specs=placed, out_specs=P("col", "row", None), check_vma=False
    )
```

```python
import jax
import jax.numpy as jnp
from jax import lax
from jax.experimental import pallas as pl
from jax.experimental.pallas import tpu as pltpu
from jax.sharding import PartitionSpec as P

EPS = 1e-05
N_ROW, N_COL = 8, 16
N_DEV = N_ROW * N_COL
NI, NK, CH = 192, 96, 128
PARTS = 3
IP = NI // PARTS
TP = NK // 2
F32, BF16 = jnp.float32, jnp.bfloat16
MESH = pl.DeviceIdType.MESH


def coords():
    row, col = lax.axis_index("row"), lax.axis_index("col")
    return (col // 8) * 2 + row % 2, row // 2, (col // 2) % 4, col % 2


def each_peer(fn, unroll=1):
    x, y, z, core = coords()
    first = ((x * 16 + y * 4 + z) * 5 + core * 64) % (N_DEV - 1)

    def body(s, _):
        t = s + first
        t = jnp.where(t >= N_DEV - 1, t - (N_DEV - 2), t + 1)
        px, py, pz, pc = (x + t) & 3, (y + (t >> 2)) & 3, (z + (t >> 4)) & 3, (core + (t >> 6)) & 1
        fn(py * 2 + (px & 1), (px >> 1) * 8 + pz * 2 + pc)
        return 0

    lax.fori_loop(0, N_DEV - 1, body, 0, unroll=unroll)


def send_part(src, dst, part, send_sem, recv_sem, start=0, size=TP, unroll=1):
    me = lax.axis_index("row") * N_COL + lax.axis_index("col")
    rows = pl.ds(start, size)

    def send(row, col):
        pltpu.make_async_remote_copy(
            src_ref=src.at[part, row * N_COL + col, rows],
            dst_ref=dst.at[part, me, rows],
            send_sem=send_sem.at[part],
            recv_sem=recv_sem.at[part],
            device_id={"row": row, "col": col},
            device_id_type=MESH,
        ).start()

    each_peer(send, unroll)
    dst[part, me, rows] = src[part, me, rows]


def wait_part(ref, part, sem, start=0, size=TP):
    whole = ref.at[part, pl.ds(0, N_DEV - 1), pl.ds(start, size)]
    pltpu.make_async_copy(whole, whole, sem.at[part]).wait()


def loop(n, body, unroll=1):
    lax.fori_loop(0, n, lambda i, c: (body(i), c)[1], 0, unroll=unroll)


def low_lanes(shape):
    return lax.broadcasted_iota(jnp.int32, shape, len(shape) - 1) < 64


def swap_halves(a, b):
    low = low_lanes(a.shape)
    return jnp.where(low, a, pltpu.roll(b, 64, 1)), jnp.where(low, pltpu.roll(a, 64, 1), b)


def kernel(
    z_hbm, mask_v, mask_s, gain, bias, w_l, w_lg, w_r, w_rg, w_og, og_s, ob_s, w_o,
    out_hbm,
    zb, nb, n32, s32, wt, send_r, send_l, recv_r, recv_l, right_t, left, recv_t, ob,
    z_sem, out_sem, rs, rr, ls, lr, ts, tr, tr2,
):
    row, col = lax.axis_index("row"), lax.axis_index("col")
    barrier = pltpu.get_barrier_semaphore()

    def load(p):
        return pltpu.make_async_copy(z_hbm.at[pl.ds(p * IP, IP)], zb.at[p], z_sem.at[p])

    for p in range(PARTS):
        load(p).start()
    each_peer(
        lambda r, c: pl.semaphore_signal(barrier, inc=1, device_id={"row": r, "col": c}, device_id_type=MESH), 4
    )

    wt[0] = w_r[...].T
    wt[1] = (w_rg[...].astype(F32) * 0.5).astype(BF16).T
    wt[2] = w_l[...].T
    wt[3] = (w_lg[...].astype(F32) * 0.5).astype(BF16).T

    def normed(v):
        v = v.astype(F32)
        mean = jnp.mean(v, axis=-1, keepdims=True)
        c = v - mean
        var = jnp.mean(c * c, axis=-1, keepdims=True)
        return c * lax.rsqrt(var + EPS) * gain[...] + bias[...]

    def normalise(p, start=0, size=TP):
        if size == TP:

            def body(i):
                v = zb[p, pl.ds(i * 2, 2)].reshape(2 * NK, CH)
                n32[pl.ds(pl.multiple_of(i * 2 * NK, 2 * NK), 2 * NK), :] = normed(v)

            loop(IP // 2, body, 4)
        else:

            def body(i):
                v = [zb[p, pl.ds(i * 4, 4), pl.ds(k, size)].reshape(4 * size, CH) for k in (start, start + TP)]
                n = normed(jnp.concatenate(v, axis=0)).reshape(8, size, CH)
                for e in range(8):
                    at = (i * 4 + e % 4) * NK + start + e // 4 * TP
                    n32[pl.ds(pl.multiple_of(at, 8), size), :] = n[e]

            loop(IP // 4, body, 4)

        def tile(t):
            t = start + t
            nb[p, t, 0:64] = n32[pl.ds(t, 64, stride=NK), :].astype(BF16)
            nb[p, t, 64:128] = n32[pl.ds(TP + t, 64, stride=NK), :].astype(BF16)

        loop(size, tile, 4)

    def project(p, which, send, start=0, size=TP):
        weights = wt[2 * which : 2 * which + 2].reshape(2 * CH, CH)
        group = 3 * row + p
        low = low_lanes((1, 128))
        m = mask_v[pl.ds(group // 2, 1), :].astype(F32) * 0.5
        other = pltpu.roll(m, 64, 1)
        first = jnp.where(group % 2 == 0, m, other)
        second = jnp.where(group % 2 == 0, other, m)
        lanes = jnp.where(low, first, second)

        def mask(t):
            k = col * NK + t
            return lanes * jnp.where(low, mask_s[k].astype(F32), mask_s[k + TP].astype(F32))

        def pair(i):
            t = start + i * 2
            rhs = nb[p, pl.ds(t, 2)].reshape(256, CH)
            both = lax.dot_general(weights, rhs, (((1,), (1,)), ((), ())), preferred_element_type=F32)
            gated = (jnp.tanh(both[CH:]) + 1.0) * both[:CH]
            s32[pl.ds(t, CH, stride=TP), :] = gated[:, :128] * mask(t)
            s32[pl.ds(t + 1, CH, stride=TP), :] = gated[:, 128:] * mask(t + 1)

        loop(size // 2, pair, 2)

        def pack(i):
            if size == TP:
                rows = s32[pl.ds(pl.multiple_of(i * 4 * TP, 4 * TP), 4 * TP), :]
                send[p, pl.ds(i * 4, 4)] = rows.astype(BF16).reshape(4, TP, 128)
            else:
                for e in range(4):
                    rows = s32[pl.ds(pl.multiple_of((i * 4 + e) * TP + start, 16), size), :]
                    send[p, i * 4 + e, start : start + size] = rows.astype(BF16)

        loop(CH // 4, pack, 2)

    def gate(p):
        def body(i):
            t = i * 2
            v = nb[p, pl.ds(t, 2)].reshape(256, CH)
            g = jnp.dot(v, w_og[...], preferred_element_type=F32)
            nb[p, pl.ds(t, 2)] = (0.5 * jnp.tanh(0.5 * g) + 0.5).astype(BF16).reshape(2, 128, CH)

        loop(TP // 2, body, 2)

    def two_rows(ref, p, y, q):
        a = ref[p, pl.ds((2 * y) * N_COL + q, 4)].astype(F32).reshape(4 * TP, 128)
        b = ref[p, pl.ds((2 * y + 1) * N_COL + q, 4)].astype(F32).reshape(4 * TP, 128)
        h0, h1 = swap_halves(a, b)
        both = jnp.concatenate([h0.reshape(4, 1, TP, 128), h1.reshape(4, 1, TP, 128)], axis=1)
        return both.reshape(4 * NK, 128).astype(BF16)

    def take_right(p):
        def body(i):
            y, q = i // 4, i % 4 * 4
            tile = two_rows(recv_r, p, y, q).T
            lane = pl.ds(pl.multiple_of(q * NK, 128), 4 * NK)
            for x in range(2):
                at = pl.multiple_of((2 * y + x) * NI + p * IP, IP)
                right_t[pl.ds(at, IP), lane] = tile[x * 64 : (x + 1) * 64]

        loop(16, body)

    def take_left(p):
        def body(i):
            y, q = i // 4, i % 4 * 4
            left[y, pl.ds(pl.multiple_of(q * NK, 128), 4 * NK), :] = two_rows(recv_l, p, y, q)

        loop(16, body)

    def product(s):
        def body(i):
            y, h = i // 4 * 2, i % 4
            rows = right_t[pl.ds(pl.multiple_of(h * 384, 384), 384), :]
            cols = jnp.concatenate([left[y], left[y + 1]], axis=1)
            tri = jnp.dot(rows, cols, preferred_element_type=F32)
            for x in range(2):
                both = tri[:, x * 128 : (x + 1) * 128].reshape(4, 2, TP, 128)
                e = swap_halves(both[:, 0].reshape(4 * TP, 128), both[:, 1].reshape(4 * TP, 128))
                for r in range(2):
                    slot = (2 * (y + x) + r) * N_COL + h * 4
                    send_r[s, pl.ds(slot, 4)] = e[r].astype(BF16).reshape(4, TP, 128)

        loop(8, body)

    def finish(s, start=0, size=TP):
        slot = s % 2
        step = 16

        def norm(g):
            at = pl.multiple_of(start + g * 16, 16)
            rows = pl.ds(at, 16)

            def some(i):
                return recv_t[s, pl.ds(i * step, step), rows, :].astype(F32)

            zero = jnp.zeros((16, 128), F32)
            mean = lax.fori_loop(0, CH // step, lambda i, a: a + jnp.sum(some(i), axis=0), zero) * (1 / CH)

            def square(i, a):
                c = some(i) - mean[None]
                return a + jnp.sum(c * c, axis=0)

            var = lax.fori_loop(0, CH // step, square, zero) * (1 / CH)
            scale = lax.rsqrt(var + EPS)

            def put(i):
                c = some(i) - mean[None]
                for e in range(step):
                    ch = i * step + e
                    s32[pl.ds(pl.multiple_of(ch * TP + at, 16), 16), :] = c[e] * scale * og_s[ch] + ob_s[ch]

            loop(CH // step, put)

        loop(size // 16, norm)

        def tile(i):
            t = start + i
            v = s32[pl.ds(t, CH, stride=TP), :].astype(BF16)
            proj = jnp.dot(v.T, w_o[...], preferred_element_type=F32)
            out = (proj * nb[s, t].astype(F32)).astype(BF16)
            ob[slot, t] = out[:64]
            ob[slot, t + TP] = out[64:]

        loop(size, tile, 4)

    def store(s):
        return pltpu.make_async_copy(ob.at[s % 2], out_hbm.at[:, pl.ds(s * IP, IP)], out_sem.at[s % 2])

    load(0).wait()
    for start, size in ((0, 16), (16, 32)):
        normalise(0, start, size)
        project(0, 0, send_r, start, size)
        if start == 0:
            pl.semaphore_wait(barrier, N_DEV - 1)
        send_part(send_r, recv_r, 0, rs, rr, start, size, 4)
    for p in range(1, PARTS):
        load(p).wait()
        normalise(p)
        project(p, 0, send_r)
        send_part(send_r, recv_r, p, rs, rr)
    for p in range(PARTS):
        project(p, 1, send_l)
        send_part(send_l, recv_l, p, ls, lr)
    for p in range(PARTS):
        gate(p)
    for p in range(PARTS):
        wait_part(recv_r, p, rr)
        take_right(p)
    last = PARTS - 1
    for p in range(PARTS):
        wait_part(send_r, p, rs)
        wait_part(recv_l, p, lr)
        take_left(p)
        product(p)
        if p < last:
            send_part(send_r, recv_t, p, ts, tr)
        else:
            send_part(send_r, recv_t, p, ts, tr, 0, 32)
            send_part(send_r, recv_t, p, ts, tr2, 32, 16)
    for p in range(last):
        wait_part(recv_t, p, tr)
        finish(p)
        store(p).start()
    store(last - 2).wait()
    wait_part(recv_t, last, tr, 0, 32)
    finish(last, 0, 32)
    wait_part(recv_t, last, tr2, 32, 16)
    finish(last, 32, 16)
    store(last).start()
    for p in range(PARTS):
        wait_part(send_l, p, ls)
        wait_part(send_r, p, ts)
    store(last - 1).wait()
    store(last).wait()


def on_device(
    pair_rep, res_mask, norm_gain, norm_bias, w_left, w_left_gate, w_right, w_right_gate, w_out_gate,
    out_gain, out_bias, w_out,
):
    vmem = pl.BlockSpec(memory_space=pltpu.VMEM)
    smem = pl.BlockSpec(memory_space=pltpu.SMEM)
    hbm = pl.BlockSpec(memory_space=pl.ANY)
    dma = pltpu.SemaphoreType.DMA
    slots = pltpu.VMEM((PARTS, N_DEV, TP, 128), BF16)
    return pl.pallas_call(
        kernel,
        out_shape=jax.ShapeDtypeStruct((NK, NI, CH), BF16),
        in_specs=[hbm, vmem, smem] + [vmem] * 7 + [smem, smem, vmem],
        out_specs=hbm,
        scratch_shapes=[
            pltpu.VMEM((PARTS, IP, NK, CH), BF16),
            pltpu.VMEM((PARTS, TP, 128, CH), BF16),
            pltpu.VMEM((IP * NK, CH), F32),
            pltpu.VMEM((CH * TP, 128), F32),
            pltpu.VMEM((4, CH, CH), BF16),
            slots, slots, slots, slots,
            pltpu.VMEM((N_COL * NK, N_COL * NK), BF16),
            pltpu.VMEM((4, N_COL * NK, 128), BF16),
            slots,
            pltpu.VMEM((2, NK, IP, CH), BF16),
            dma((PARTS,)), dma((2,)),
            dma((PARTS,)), dma((PARTS,)), dma((PARTS,)), dma((PARTS,)), dma((PARTS,)), dma((PARTS,)), dma((PARTS,)),
        ],
        compiler_params=pltpu.CompilerParams(
            collective_id=0, has_side_effects=True, vmem_limit_bytes=60 << 20
        ),
        cost_estimate=pl.CostEstimate(flops=11 * 10**9, bytes_accessed=10**7, transcendentals=7 * 10**6),
    )(
        pair_rep, res_mask.reshape(12, 128), res_mask, norm_gain[None], norm_bias[None], w_left, w_left_gate, w_right,
        w_right_gate, w_out_gate, out_gain, out_bias, w_out,
    )


def solution(mesh):
    placed = (P("row", "col", None), P(), P(), P(), P(), P(), P(), P(), P(), P(), P(), P())
    return jax.shard_map(
        on_device, mesh=mesh, in_specs=placed, out_specs=P("col", "row", None), check_vma=False
    )
```

```python
import jax
import jax.numpy as jnp
from jax import lax
from jax.experimental import pallas as pl
from jax.experimental.pallas import tpu as pltpu
from jax.sharding import PartitionSpec as P

EPS = 1e-05
N_ROW, N_COL = 8, 16
N_DEV = N_ROW * N_COL
NI, NK, CH = 192, 96, 128
PARTS = 3
IP = NI // PARTS
TP = NK // 2
F32, BF16 = jnp.float32, jnp.bfloat16
MESH = pl.DeviceIdType.MESH


def coords():
    row, col = lax.axis_index("row"), lax.axis_index("col")
    return (col // 8) * 2 + row % 2, row // 2, (col // 2) % 4, col % 2


def each_peer(fn, unroll=1):
    x, y, z, core = coords()
    first = ((x * 16 + y * 4 + z) * 5 + core * 64) % (N_DEV - 1)

    def body(s, _):
        t = s + first
        t = jnp.where(t >= N_DEV - 1, t - (N_DEV - 2), t + 1)
        px, py, pz, pc = (x + t) & 3, (y + (t >> 2)) & 3, (z + (t >> 4)) & 3, (core + (t >> 6)) & 1
        fn(py * 2 + (px & 1), (px >> 1) * 8 + pz * 2 + pc)
        return 0

    lax.fori_loop(0, N_DEV - 1, body, 0, unroll=unroll)


def send_part(src, dst, part, send_sem, recv_sem, start=0, size=TP, unroll=1):
    me = lax.axis_index("row") * N_COL + lax.axis_index("col")
    rows = pl.ds(start, size)

    def send(row, col):
        pltpu.make_async_remote_copy(
            src_ref=src.at[part, row * N_COL + col, rows],
            dst_ref=dst.at[part, me, rows],
            send_sem=send_sem.at[part],
            recv_sem=recv_sem.at[part],
            device_id={"row": row, "col": col},
            device_id_type=MESH,
        ).start()

    each_peer(send, unroll)
    dst[part, me, rows] = src[part, me, rows]


def wait_part(ref, part, sem, start=0, size=TP):
    whole = ref.at[part, pl.ds(0, N_DEV - 1), pl.ds(start, size)]
    pltpu.make_async_copy(whole, whole, sem.at[part]).wait()


def loop(n, body, unroll=1):
    lax.fori_loop(0, n, lambda i, c: (body(i), c)[1], 0, unroll=unroll)


def low_lanes(shape):
    return lax.broadcasted_iota(jnp.int32, shape, len(shape) - 1) < 64


def swap_halves(a, b):
    low = low_lanes(a.shape)
    return jnp.where(low, a, pltpu.roll(b, 64, 1)), jnp.where(low, pltpu.roll(a, 64, 1), b)


def kernel(
    z_hbm, mask_v_hbm, mask_s_hbm, gain_hbm, bias_hbm, w_r_hbm, w_rg_hbm, w_l_hbm, w_lg_hbm, w_og_hbm, w_o_hbm,
    og_hbm, ob_hbm,
    out,
    zb, nb, n32, s32, wt, send_r, send_l, recv_r, recv_l, right_t, left, recv_t,
    mask_v, gain, bias, weights_in, mask_s, og_s, ob_s,
    z_sem, in_sem, rs, rr, ls, lr, ts, tr, tr2,
):
    row, col = lax.axis_index("row"), lax.axis_index("col")
    barrier = pltpu.get_barrier_semaphore()

    def load(p):
        return pltpu.make_async_copy(z_hbm.at[pl.ds(p * IP, IP)], zb.at[p], z_sem.at[p])

    load(0).start()
    small = [(gain_hbm, gain), (bias_hbm, bias), (mask_v_hbm, mask_v), (mask_s_hbm, mask_s), (og_hbm, og_s), (ob_hbm, ob_s)]
    for i, ref in enumerate((w_r_hbm, w_rg_hbm, w_l_hbm, w_lg_hbm, w_og_hbm, w_o_hbm)):
        small.append((ref, weights_in.at[i]))
    small = [pltpu.make_async_copy(a, b, in_sem.at[i]) for i, (a, b) in enumerate(small)]
    for copy in small:
        copy.start()
    for p in range(1, PARTS):
        load(p).start()
    each_peer(
        lambda r, c: pl.semaphore_signal(barrier, inc=1, device_id={"row": r, "col": c}, device_id_type=MESH), 16
    )

    for copy in small:
        copy.wait()
    for i in range(4):
        wt[i] = (weights_in[i].astype(F32) * (0.5 if i % 2 else 1.0)).astype(BF16).T

    def normed(v):
        v = v.astype(F32)
        mean = jnp.mean(v, axis=-1, keepdims=True)
        c = v - mean
        var = jnp.mean(c * c, axis=-1, keepdims=True)
        return c * lax.rsqrt(var + EPS) * gain[...] + bias[...]

    def normalise(p, start=0, size=TP):
        if size == TP:

            def body(i):
                v = zb[p, pl.ds(i * 2, 2)].reshape(2 * NK, CH)
                n32[pl.ds(pl.multiple_of(i * 2 * NK, 2 * NK), 2 * NK), :] = normed(v)

            loop(IP // 2, body, 4)
        else:

            def body(i):
                v = [zb[p, pl.ds(i * 4, 4), pl.ds(k, size)].reshape(4 * size, CH) for k in (start, start + TP)]
                n = normed(jnp.concatenate(v, axis=0)).reshape(8, size, CH)
                for e in range(8):
                    at = (i * 4 + e % 4) * NK + start + e // 4 * TP
                    n32[pl.ds(pl.multiple_of(at, 8), size), :] = n[e]

            loop(IP // 4, body, 4)

        def tile(t):
            t = start + t
            nb[p, t, 0:64] = n32[pl.ds(t, 64, stride=NK), :].astype(BF16)
            nb[p, t, 64:128] = n32[pl.ds(TP + t, 64, stride=NK), :].astype(BF16)

        loop(size, tile, 4)

    def project(p, which, send, start=0, size=TP):
        weights = wt[2 * which : 2 * which + 2].reshape(2 * CH, CH)
        group = 3 * row + p
        low = low_lanes((1, 128))
        m = mask_v[pl.ds(group // 2, 1), :].astype(F32) * 0.5
        other = pltpu.roll(m, 64, 1)
        first = jnp.where(group % 2 == 0, m, other)
        second = jnp.where(group % 2 == 0, other, m)
        lanes = jnp.where(low, first, second)

        def mask(t):
            k = col * NK + t
            return lanes * jnp.where(low, mask_s[k].astype(F32), mask_s[k + TP].astype(F32))

        def pair(i):
            t = start + i * 2
            rhs = nb[p, pl.ds(t, 2)].reshape(256, CH)
            both = lax.dot_general(weights, rhs, (((1,), (1,)), ((), ())), preferred_element_type=F32)
            gated = (jnp.tanh(both[CH:]) + 1.0) * both[:CH]
            s32[pl.ds(t, CH, stride=TP), :] = gated[:, :128] * mask(t)
            s32[pl.ds(t + 1, CH, stride=TP), :] = gated[:, 128:] * mask(t + 1)

        loop(size // 2, pair, 2)

        def pack(i):
            if size == TP:
                rows = s32[pl.ds(pl.multiple_of(i * 4 * TP, 4 * TP), 4 * TP), :]
                send[p, pl.ds(i * 4, 4)] = rows.astype(BF16).reshape(4, TP, 128)
            else:
                for e in range(4):
                    rows = s32[pl.ds(pl.multiple_of((i * 4 + e) * TP + start, 16), size), :]
                    send[p, i * 4 + e, start : start + size] = rows.astype(BF16)

        loop(CH // 4, pack, 2)

    def gate(p):
        def body(i):
            t = i * 2
            v = nb[p, pl.ds(t, 2)].reshape(256, CH)
            g = jnp.dot(v, weights_in[4], preferred_element_type=F32)
            nb[p, pl.ds(t, 2)] = (0.5 * jnp.tanh(0.5 * g) + 0.5).astype(BF16).reshape(2, 128, CH)

        loop(TP // 2, body, 2)

    def two_rows(ref, p, y, q):
        a = ref[p, pl.ds((2 * y) * N_COL + q, 4)].astype(F32).reshape(4 * TP, 128)
        b = ref[p, pl.ds((2 * y + 1) * N_COL + q, 4)].astype(F32).reshape(4 * TP, 128)
        h0, h1 = swap_halves(a, b)
        both = jnp.concatenate([h0.reshape(4, 1, TP, 128), h1.reshape(4, 1, TP, 128)], axis=1)
        return both.reshape(4 * NK, 128).astype(BF16)

    def take_right(p):
        def body(i):
            y, q = i // 4, i % 4 * 4
            tile = two_rows(recv_r, p, y, q).T
            lane = pl.ds(pl.multiple_of(q * NK, 128), 4 * NK)
            for x in range(2):
                at = pl.multiple_of((2 * y + x) * NI + p * IP, IP)
                right_t[pl.ds(at, IP), lane] = tile[x * 64 : (x + 1) * 64]

        loop(16, body)

    def take_left(p):
        def body(i):
            y, q = i // 4, i % 4 * 4
            left[y, pl.ds(pl.multiple_of(q * NK, 128), 4 * NK), :] = two_rows(recv_l, p, y, q)

        loop(16, body)

    def product(s):
        def body(i):
            y, h = i // 4 * 2, i % 4
            rows = right_t[pl.ds(pl.multiple_of(h * 384, 384), 384), :]
            cols = jnp.concatenate([left[y], left[y + 1]], axis=1)
            tri = jnp.dot(rows, cols, preferred_element_type=F32)
            for x in range(2):
                both = tri[:, x * 128 : (x + 1) * 128].reshape(4, 2, TP, 128)
                e = swap_halves(both[:, 0].reshape(4 * TP, 128), both[:, 1].reshape(4 * TP, 128))
                for r in range(2):
                    slot = (2 * (y + x) + r) * N_COL + h * 4
                    send_r[s, pl.ds(slot, 4)] = e[r].astype(BF16).reshape(4, TP, 128)

        loop(8, body)

    def finish(s, start=0, size=TP):
        step = 16

        def norm(g):
            at = pl.multiple_of(start + g * 16, 16)
            rows = pl.ds(at, 16)

            def some(i):
                return recv_t[s, pl.ds(i * step, step), rows, :].astype(F32)

            zero = jnp.zeros((16, 128), F32)
            mean = lax.fori_loop(0, CH // step, lambda i, a: a + jnp.sum(some(i), axis=0), zero) * (1 / CH)

            def square(i, a):
                c = some(i) - mean[None]
                return a + jnp.sum(c * c, axis=0)

            var = lax.fori_loop(0, CH // step, square, zero) * (1 / CH)
            scale = lax.rsqrt(var + EPS)

            def put(i):
                c = some(i) - mean[None]
                for e in range(step):
                    ch = i * step + e
                    s32[pl.ds(pl.multiple_of(ch * TP + at, 16), 16), :] = c[e] * scale * og_s[ch] + ob_s[ch]

            loop(CH // step, put)

        loop(size // 16, norm)

        def tile(i):
            t = start + i
            v = s32[pl.ds(t, CH, stride=TP), :].astype(BF16)
            proj = jnp.dot(v.T, weights_in[5], preferred_element_type=F32)
            update = (proj * nb[s, t].astype(F32)).astype(BF16)
            out[t, s * IP : (s + 1) * IP] = update[:64]
            out[t + TP, s * IP : (s + 1) * IP] = update[64:]

        loop(size, tile, 4)

    load(0).wait()
    for start, size in ((0, 16), (16, 32)):
        normalise(0, start, size)
        project(0, 0, send_r, start, size)
        if start == 0:
            pl.semaphore_wait(barrier, N_DEV - 1)
        send_part(send_r, recv_r, 0, rs, rr, start, size, 4)
    for p in range(1, PARTS):
        load(p).wait()
        normalise(p)
        project(p, 0, send_r)
        send_part(send_r, recv_r, p, rs, rr)
    for p in range(PARTS):
        project(p, 1, send_l)
        send_part(send_l, recv_l, p, ls, lr)
    for p in range(PARTS):
        gate(p)
    for p in range(PARTS):
        wait_part(recv_r, p, rr)
        take_right(p)
    last = PARTS - 1
    for p in range(PARTS):
        wait_part(send_r, p, rs)
        wait_part(recv_l, p, lr)
        take_left(p)
        product(p)
        if p < last:
            send_part(send_r, recv_t, p, ts, tr)
        else:
            send_part(send_r, recv_t, p, ts, tr, 0, 32)
            send_part(send_r, recv_t, p, ts, tr2, 32, 16)
    for p in range(last):
        wait_part(recv_t, p, tr)
        finish(p)
    wait_part(recv_t, last, tr, 0, 32)
    finish(last, 0, 32)
    wait_part(recv_t, last, tr2, 32, 16)
    finish(last, 32, 16)
    for p in range(PARTS):
        wait_part(send_l, p, ls)
        wait_part(send_r, p, ts)


def on_device(
    pair_rep, res_mask, norm_gain, norm_bias, w_left, w_left_gate, w_right, w_right_gate, w_out_gate,
    out_gain, out_bias, w_out,
):
    vmem = pl.BlockSpec(memory_space=pltpu.VMEM)
    hbm = pl.BlockSpec(memory_space=pltpu.HBM)
    dma = pltpu.SemaphoreType.DMA
    slots = pltpu.VMEM((PARTS, N_DEV, TP, 128), BF16)
    return pl.pallas_call(
        kernel,
        out_shape=pltpu.VMEM((NK, NI, CH), BF16),
        in_specs=[hbm] * 13,
        out_specs=vmem,
        scratch_shapes=[
            pltpu.VMEM((PARTS, IP, NK, CH), BF16),
            pltpu.VMEM((PARTS, TP, 128, CH), BF16),
            pltpu.VMEM((IP * NK + NK, CH), F32),
            pltpu.VMEM((CH * TP + TP, 128), F32),
            pltpu.VMEM((4, CH, CH), BF16),
            slots, slots, slots, slots,
            pltpu.VMEM((N_COL * NK, N_COL * NK), BF16),
            pltpu.VMEM((4, N_COL * NK, 128), BF16),
            slots,
            pltpu.VMEM((12, 128), jnp.int32),
            pltpu.VMEM((1, CH), F32),
            pltpu.VMEM((1, CH), F32),
            pltpu.VMEM((6, CH, CH), BF16),
            pltpu.SMEM((N_COL * NK,), jnp.int32),
            pltpu.SMEM((CH,), F32),
            pltpu.SMEM((CH,), F32),
            dma((PARTS,)), dma((12,)),
            dma((PARTS,)), dma((PARTS,)), dma((PARTS,)), dma((PARTS,)), dma((PARTS,)), dma((PARTS,)), dma((PARTS,)),
        ],
        compiler_params=pltpu.CompilerParams(
            collective_id=0, has_side_effects=True, vmem_limit_bytes=58 << 20
        ),
        cost_estimate=pl.CostEstimate(flops=11 * 10**9, bytes_accessed=10**7, transcendentals=7 * 10**6),
    )(
        pair_rep, res_mask.reshape(12, 128), res_mask, norm_gain[None], norm_bias[None], w_right, w_right_gate, w_left,
        w_left_gate, w_out_gate, w_out, out_gain, out_bias,
    )


def solution(mesh):
    placed = (P("row", "col", None), P(), P(), P(), P(), P(), P(), P(), P(), P(), P(), P())
    return jax.shard_map(
        on_device, mesh=mesh, in_specs=placed, out_specs=P("col", "row", None), check_vma=False
    )
```

```python
import jax
import jax.numpy as jnp
from jax import lax
from jax.experimental import pallas as pl
from jax.experimental.pallas import tpu as pltpu
from jax.sharding import PartitionSpec as P

EPS = 1e-05
N_ROW, N_COL = 8, 16
N_DEV = N_ROW * N_COL
NI, NK, CH = 192, 96, 128
PARTS = 3
IP = NI // PARTS
TP = NK // 2
F32, BF16 = jnp.float32, jnp.bfloat16
MESH = pl.DeviceIdType.MESH


def coords():
    row, col = lax.axis_index("row"), lax.axis_index("col")
    return (col // 8) * 2 + row % 2, row // 2, (col // 2) % 4, col % 2


def each_peer(fn, unroll=1):
    x, y, z, core = coords()
    first = ((x * 16 + y * 4 + z) * 5 + core * 64) % (N_DEV - 1)

    def body(s, _):
        t = s + first
        t = jnp.where(t >= N_DEV - 1, t - (N_DEV - 2), t + 1)
        px, py, pz, pc = (x + t) & 3, (y + (t >> 2)) & 3, (z + (t >> 4)) & 3, (core + (t >> 6)) & 1
        fn(py * 2 + (px & 1), (px >> 1) * 8 + pz * 2 + pc)
        return 0

    lax.fori_loop(0, N_DEV - 1, body, 0, unroll=unroll)


def send_part(src, dst, part, send_sem, recv_sem, start=0, size=TP, unroll=1):
    me = lax.axis_index("row") * N_COL + lax.axis_index("col")
    rows = pl.ds(start, size)

    def send(row, col):
        pltpu.make_async_remote_copy(
            src_ref=src.at[part, row * N_COL + col, rows],
            dst_ref=dst.at[part, me, rows],
            send_sem=send_sem.at[part],
            recv_sem=recv_sem.at[part],
            device_id={"row": row, "col": col},
            device_id_type=MESH,
        ).start()

    each_peer(send, unroll)
    dst[part, me, rows] = src[part, me, rows]


def wait_part(ref, part, sem, start=0, size=TP):
    whole = ref.at[part, pl.ds(0, N_DEV - 1), pl.ds(start, size)]
    pltpu.make_async_copy(whole, whole, sem.at[part]).wait()


def loop(n, body, unroll=1):
    lax.fori_loop(0, n, lambda i, c: (body(i), c)[1], 0, unroll=unroll)


def low_lanes(shape):
    return lax.broadcasted_iota(jnp.int32, shape, len(shape) - 1) < 64


def swap_halves(a, b):
    low = low_lanes(a.shape)
    return jnp.where(low, a, pltpu.roll(b, 64, 1)), jnp.where(low, pltpu.roll(a, 64, 1), b)


def kernel(
    z_hbm, mask_v_hbm, mask_s_hbm, gain_hbm, bias_hbm, w_r_hbm, w_rg_hbm, w_l_hbm, w_lg_hbm, w_og_hbm, w_o_hbm,
    og_hbm, ob_hbm,
    out,
    zb, nb, n32, s32, wt, send_r, send_l, recv_r, recv_l, right_t, left, recv_t,
    mask_v, gain, bias, weights_in, mask_s, og_s, ob_s,
    z_sem, in_sem, rs, rr, ls, lr, ts, tr, tr2,
):
    row, col = lax.axis_index("row"), lax.axis_index("col")
    barrier = pltpu.get_barrier_semaphore()

    def load(p):
        return pltpu.make_async_copy(z_hbm.at[pl.ds(p * IP, IP)], zb.at[p], z_sem.at[p])

    load(0).start()
    small = [(gain_hbm, gain), (bias_hbm, bias), (mask_v_hbm, mask_v), (mask_s_hbm, mask_s), (og_hbm, og_s), (ob_hbm, ob_s)]
    for i, ref in enumerate((w_r_hbm, w_rg_hbm, w_l_hbm, w_lg_hbm, w_og_hbm, w_o_hbm)):
        small.append((ref, weights_in.at[i]))
    small = [pltpu.make_async_copy(a, b, in_sem.at[i]) for i, (a, b) in enumerate(small)]
    for copy in small:
        copy.start()
    for p in range(1, PARTS):
        load(p).start()
    each_peer(
        lambda r, c: pl.semaphore_signal(barrier, inc=1, device_id={"row": r, "col": c}, device_id_type=MESH), 16
    )

    for copy in small:
        copy.wait()
    for i in range(4):
        wt[i] = (weights_in[i].astype(F32) * (0.5 if i % 2 else 1.0)).astype(BF16).T

    def normed(v):
        v = v.astype(F32)
        mean = jnp.mean(v, axis=-1, keepdims=True)
        c = v - mean
        var = jnp.mean(c * c, axis=-1, keepdims=True)
        return c * lax.rsqrt(var + EPS) * gain[...] + bias[...]

    def normalise(p, start=0, size=TP):
        if size == TP:

            def body(i):
                v = zb[p, pl.ds(i * 2, 2)].reshape(2 * NK, CH)
                n32[pl.ds(pl.multiple_of(i * 2 * NK, 2 * NK), 2 * NK), :] = normed(v)

            loop(IP // 2, body, 4)
        else:

            def body(i):
                v = [zb[p, pl.ds(i * 4, 4), pl.ds(k, size)].reshape(4 * size, CH) for k in (start, start + TP)]
                n = normed(jnp.concatenate(v, axis=0)).reshape(8, size, CH)
                for e in range(8):
                    at = (i * 4 + e % 4) * NK + start + e // 4 * TP
                    n32[pl.ds(pl.multiple_of(at, 8), size), :] = n[e]

            loop(IP // 4, body, 4)

        def tile(t):
            t = start + t
            nb[p, t, 0:64] = n32[pl.ds(t, 64, stride=NK), :].astype(BF16)
            nb[p, t, 64:128] = n32[pl.ds(TP + t, 64, stride=NK), :].astype(BF16)

        loop(size, tile, 4)

    def project(p, which, send, start=0, size=TP):
        weights = wt[2 * which : 2 * which + 2].reshape(2 * CH, CH)
        group = 3 * row + p
        low = low_lanes((1, 128))
        m = mask_v[pl.ds(group // 2, 1), :].astype(F32) * 0.5
        other = pltpu.roll(m, 64, 1)
        first = jnp.where(group % 2 == 0, m, other)
        second = jnp.where(group % 2 == 0, other, m)
        lanes = jnp.where(low, first, second)

        def mask(t):
            k = col * NK + t
            return lanes * jnp.where(low, mask_s[k].astype(F32), mask_s[k + TP].astype(F32))

        def pair(i):
            t = start + i * 2
            rhs = nb[p, pl.ds(t, 2)].reshape(256, CH)
            both = lax.dot_general(weights, rhs, (((1,), (1,)), ((), ())), preferred_element_type=F32)
            gated = (jnp.tanh(both[CH:]) + 1.0) * both[:CH]
            s32[pl.ds(t, CH, stride=TP), :] = gated[:, :128] * mask(t)
            s32[pl.ds(t + 1, CH, stride=TP), :] = gated[:, 128:] * mask(t + 1)

        loop(size // 2, pair, 4)

        def pack(i):
            if size == TP:
                rows = s32[pl.ds(pl.multiple_of(i * 4 * TP, 4 * TP), 4 * TP), :]
                send[p, pl.ds(i * 4, 4)] = rows.astype(BF16).reshape(4, TP, 128)
            else:
                for e in range(4):
                    rows = s32[pl.ds(pl.multiple_of((i * 4 + e) * TP + start, 16), size), :]
                    send[p, i * 4 + e, start : start + size] = rows.astype(BF16)

        loop(CH // 4, pack, 2)

    def gate(p):
        def body(i):
            t = i * 2
            v = nb[p, pl.ds(t, 2)].reshape(256, CH)
            g = jnp.dot(v, weights_in[4], preferred_element_type=F32)
            nb[p, pl.ds(t, 2)] = (0.5 * jnp.tanh(0.5 * g) + 0.5).astype(BF16).reshape(2, 128, CH)

        loop(TP // 2, body, 2)

    def two_rows(ref, p, y, q):
        a = ref[p, pl.ds((2 * y) * N_COL + q, 4)].astype(F32).reshape(4 * TP, 128)
        b = ref[p, pl.ds((2 * y + 1) * N_COL + q, 4)].astype(F32).reshape(4 * TP, 128)
        h0, h1 = swap_halves(a, b)
        both = jnp.concatenate([h0.reshape(4, 1, TP, 128), h1.reshape(4, 1, TP, 128)], axis=1)
        return both.reshape(4 * NK, 128).astype(BF16)

    def take_right(p):
        def body(i):
            y, q = i // 4, i % 4 * 4
            tile = two_rows(recv_r, p, y, q).T
            lane = pl.ds(pl.multiple_of(q * NK, 128), 4 * NK)
            for x in range(2):
                at = pl.multiple_of((2 * y + x) * NI + p * IP, IP)
                right_t[pl.ds(at, IP), lane] = tile[x * 64 : (x + 1) * 64]

        loop(16, body)

    def take_left(p):
        def body(i):
            y, q = i // 4, i % 4 * 4
            left[y, pl.ds(pl.multiple_of(q * NK, 128), 4 * NK), :] = two_rows(recv_l, p, y, q)

        loop(16, body)

    def product(s):
        def body(i):
            y, h = i // 4 * 2, i % 4
            rows = right_t[pl.ds(pl.multiple_of(h * 384, 384), 384), :]
            cols = jnp.concatenate([left[y], left[y + 1]], axis=1)
            tri = jnp.dot(rows, cols, preferred_element_type=F32)
            for x in range(2):
                both = tri[:, x * 128 : (x + 1) * 128].reshape(4, 2, TP, 128)
                e = swap_halves(both[:, 0].reshape(4 * TP, 128), both[:, 1].reshape(4 * TP, 128))
                for r in range(2):
                    slot = (2 * (y + x) + r) * N_COL + h * 4
                    send_r[s, pl.ds(slot, 4)] = e[r].astype(BF16).reshape(4, TP, 128)

        loop(8, body)

    def finish(s, start=0, size=TP):
        step = 16

        def norm(g):
            at = pl.multiple_of(start + g * 16, 16)
            rows = pl.ds(at, 16)

            def some(i):
                return recv_t[s, pl.ds(i * step, step), rows, :].astype(F32)

            zero = jnp.zeros((16, 128), F32)
            mean = lax.fori_loop(0, CH // step, lambda i, a: a + jnp.sum(some(i), axis=0), zero) * (1 / CH)

            def square(i, a):
                c = some(i) - mean[None]
                return a + jnp.sum(c * c, axis=0)

            var = lax.fori_loop(0, CH // step, square, zero) * (1 / CH)
            scale = lax.rsqrt(var + EPS)

            def put(i):
                c = some(i) - mean[None]
                for e in range(step):
                    ch = i * step + e
                    s32[pl.ds(pl.multiple_of(ch * TP + at, 16), 16), :] = c[e] * scale * og_s[ch] + ob_s[ch]

            loop(CH // step, put)

        loop(size // 16, norm)

        def tile(i):
            t = start + i
            v = s32[pl.ds(t, CH, stride=TP), :].astype(BF16)
            proj = jnp.dot(v.T, weights_in[5], preferred_element_type=F32)
            update = (proj * nb[s, t].astype(F32)).astype(BF16)
            out[t, s * IP : (s + 1) * IP] = update[:64]
            out[t + TP, s * IP : (s + 1) * IP] = update[64:]

        loop(size, tile, 16)

    load(0).wait()
    for start, size in ((0, 16), (16, 32)):
        normalise(0, start, size)
        project(0, 0, send_r, start, size)
        if start == 0:
            pl.semaphore_wait(barrier, N_DEV - 1)
        send_part(send_r, recv_r, 0, rs, rr, start, size, 4)
    for p in range(1, PARTS):
        load(p).wait()
        normalise(p)
        project(p, 0, send_r)
        send_part(send_r, recv_r, p, rs, rr)
    for p in range(PARTS):
        project(p, 1, send_l)
        send_part(send_l, recv_l, p, ls, lr)
    for p in range(PARTS):
        gate(p)
    for p in range(PARTS):
        wait_part(recv_r, p, rr)
        take_right(p)
    last = PARTS - 1
    for p in range(PARTS):
        wait_part(send_r, p, rs)
        wait_part(recv_l, p, lr)
        take_left(p)
        product(p)
        if p < last:
            send_part(send_r, recv_t, p, ts, tr)
        else:
            send_part(send_r, recv_t, p, ts, tr, 0, 32)
            send_part(send_r, recv_t, p, ts, tr2, 32, 16)
    for p in range(last):
        wait_part(recv_t, p, tr)
        finish(p)
    wait_part(recv_t, last, tr, 0, 32)
    finish(last, 0, 32)
    wait_part(recv_t, last, tr2, 32, 16)
    finish(last, 32, 16)
    for p in range(PARTS):
        wait_part(send_l, p, ls)
        wait_part(send_r, p, ts)


def on_device(
    pair_rep, res_mask, norm_gain, norm_bias, w_left, w_left_gate, w_right, w_right_gate, w_out_gate,
    out_gain, out_bias, w_out,
):
    vmem = pl.BlockSpec(memory_space=pltpu.VMEM)
    hbm = pl.BlockSpec(memory_space=pltpu.HBM)
    dma = pltpu.SemaphoreType.DMA
    slots = pltpu.VMEM((PARTS, N_DEV, TP, 128), BF16)
    return pl.pallas_call(
        kernel,
        out_shape=pltpu.VMEM((NK, NI, CH), BF16),
        in_specs=[hbm] * 13,
        out_specs=vmem,
        scratch_shapes=[
            pltpu.VMEM((PARTS, IP, NK, CH), BF16),
            pltpu.VMEM((PARTS, TP, 128, CH), BF16),
            pltpu.VMEM((IP * NK + NK, CH), F32),
            pltpu.VMEM((CH * TP + TP, 128), F32),
            pltpu.VMEM((4, CH, CH), BF16),
            slots, slots, slots, slots,
            pltpu.VMEM((N_COL * NK, N_COL * NK), BF16),
            pltpu.VMEM((4, N_COL * NK, 128), BF16),
            slots,
            pltpu.VMEM((12, 128), jnp.int32),
            pltpu.VMEM((1, CH), F32),
            pltpu.VMEM((1, CH), F32),
            pltpu.VMEM((6, CH, CH), BF16),
            pltpu.SMEM((N_COL * NK,), jnp.int32),
            pltpu.SMEM((CH,), F32),
            pltpu.SMEM((CH,), F32),
            dma((PARTS,)), dma((12,)),
            dma((PARTS,)), dma((PARTS,)), dma((PARTS,)), dma((PARTS,)), dma((PARTS,)), dma((PARTS,)), dma((PARTS,)),
        ],
        compiler_params=pltpu.CompilerParams(
            collective_id=0, has_side_effects=True, vmem_limit_bytes=58 << 20
        ),
        cost_estimate=pl.CostEstimate(flops=11 * 10**9, bytes_accessed=10**7, transcendentals=7 * 10**6),
    )(
        pair_rep, res_mask.reshape(12, 128), res_mask, norm_gain[None], norm_bias[None], w_right, w_right_gate, w_left,
        w_left_gate, w_out_gate, w_out, out_gain, out_bias,
    )


def solution(mesh):
    placed = (P("row", "col", None), P(), P(), P(), P(), P(), P(), P(), P(), P(), P(), P())
    return jax.shard_map(
        on_device, mesh=mesh, in_specs=placed, out_specs=P("col", "row", None), check_vma=False
    )
```

```python
import jax
import jax.numpy as jnp
from jax import lax
from jax.experimental import pallas as pl
from jax.experimental.pallas import tpu as pltpu
from jax.sharding import PartitionSpec as P

EPS = 1e-05
N_ROW, N_COL = 8, 16
N_DEV = N_ROW * N_COL
NI, NK, CH = 192, 96, 128
PARTS = 3
IP = NI // PARTS
TP = NK // 2
F32, BF16 = jnp.float32, jnp.bfloat16
MESH = pl.DeviceIdType.MESH


def coords():
    row, col = lax.axis_index("row"), lax.axis_index("col")
    return (col // 8) * 2 + row % 2, row // 2, (col // 2) % 4, col % 2


def each_peer(fn, unroll=1):
    x, y, z, core = coords()
    first = ((x * 16 + y * 4 + z) * 5 + core * 64) % (N_DEV - 1)

    def body(s, _):
        t = s + first
        t = jnp.where(t >= N_DEV - 1, t - (N_DEV - 2), t + 1)
        px, py, pz, pc = (x + t) & 3, (y + (t >> 2)) & 3, (z + (t >> 4)) & 3, (core + (t >> 6)) & 1
        fn(py * 2 + (px & 1), (px >> 1) * 8 + pz * 2 + pc)
        return 0

    lax.fori_loop(0, N_DEV - 1, body, 0, unroll=unroll)


def send_part(src, dst, part, send_sem, recv_sem, start=0, size=TP, unroll=1):
    me = lax.axis_index("row") * N_COL + lax.axis_index("col")
    rows = pl.ds(start, size)

    def send(row, col):
        pltpu.make_async_remote_copy(
            src_ref=src.at[part, row * N_COL + col, rows],
            dst_ref=dst.at[part, me, rows],
            send_sem=send_sem.at[part],
            recv_sem=recv_sem.at[part],
            device_id={"row": row, "col": col},
            device_id_type=MESH,
        ).start()

    each_peer(send, unroll)
    dst[part, me, rows] = src[part, me, rows]


def wait_part(ref, part, sem, start=0, size=TP):
    whole = ref.at[part, pl.ds(0, N_DEV - 1), pl.ds(start, size)]
    pltpu.make_async_copy(whole, whole, sem.at[part]).wait()


def loop(n, body, unroll=1):
    lax.fori_loop(0, n, lambda i, c: (body(i), c)[1], 0, unroll=unroll)


def low_lanes(shape):
    return lax.broadcasted_iota(jnp.int32, shape, len(shape) - 1) < 64


def swap_halves(a, b):
    low = low_lanes(a.shape)
    return jnp.where(low, a, pltpu.roll(b, 64, 1)), jnp.where(low, pltpu.roll(a, 64, 1), b)


def kernel(
    z_hbm, mask_v_hbm, mask_s_hbm, gain_hbm, bias_hbm, w_r_hbm, w_rg_hbm, w_l_hbm, w_lg_hbm, w_og_hbm, w_o_hbm,
    og_hbm, ob_hbm,
    out,
    zb, nb, n32, s32, wt, send_r, send_l, recv_r, recv_l, right_t, left, recv_t,
    mask_v, gain, bias, weights_in, mask_s, og_s, ob_s,
    z_sem, in_sem, rs, rr, ls, lr, ts, tr, tr2,
):
    row, col = lax.axis_index("row"), lax.axis_index("col")
    barrier = pltpu.get_barrier_semaphore()

    def load(p):
        return pltpu.make_async_copy(z_hbm.at[pl.ds(p * IP, IP)], zb.at[p], z_sem.at[p])

    load(0).start()
    small = [(gain_hbm, gain), (bias_hbm, bias), (mask_v_hbm, mask_v), (mask_s_hbm, mask_s), (og_hbm, og_s), (ob_hbm, ob_s)]
    for i, ref in enumerate((w_r_hbm, w_rg_hbm, w_l_hbm, w_lg_hbm, w_og_hbm, w_o_hbm)):
        small.append((ref, weights_in.at[i]))
    small = [pltpu.make_async_copy(a, b, in_sem.at[i]) for i, (a, b) in enumerate(small)]
    for copy in small:
        copy.start()
    for p in range(1, PARTS):
        load(p).start()
    each_peer(
        lambda r, c: pl.semaphore_signal(barrier, inc=1, device_id={"row": r, "col": c}, device_id_type=MESH), 16
    )

    for copy in small:
        copy.wait()
    for i in range(4):
        wt[i] = (weights_in[i].astype(F32) * (0.5 if i % 2 else 1.0)).astype(BF16).T

    def normed(v):
        v = v.astype(F32)
        mean = jnp.mean(v, axis=-1, keepdims=True)
        c = v - mean
        var = jnp.mean(c * c, axis=-1, keepdims=True)
        return c * lax.rsqrt(var + EPS) * gain[...] + bias[...]

    def normalise(p, start=0, size=TP):
        if size == TP:

            def body(i):
                v = zb[p, pl.ds(i * 2, 2)].reshape(2 * NK, CH)
                n32[pl.ds(pl.multiple_of(i * 2 * NK, 2 * NK), 2 * NK), :] = normed(v)

            loop(IP // 2, body, 4)
        else:

            def body(i):
                v = [zb[p, pl.ds(i * 4, 4), pl.ds(k, size)].reshape(4 * size, CH) for k in (start, start + TP)]
                n = normed(jnp.concatenate(v, axis=0)).reshape(8, size, CH)
                for e in range(8):
                    at = (i * 4 + e % 4) * NK + start + e // 4 * TP
                    n32[pl.ds(pl.multiple_of(at, 8), size), :] = n[e]

            loop(IP // 4, body, 4)

        def tile(t):
            t = start + t
            nb[p, t, 0:64] = n32[pl.ds(t, 64, stride=NK), :].astype(BF16)
            nb[p, t, 64:128] = n32[pl.ds(TP + t, 64, stride=NK), :].astype(BF16)

        loop(size, tile, 4)

    def project(p, which, send, start=0, size=TP):
        weights = wt[2 * which : 2 * which + 2].reshape(2 * CH, CH)
        group = 3 * row + p
        low = low_lanes((1, 128))
        m = mask_v[pl.ds(group // 2, 1), :].astype(F32) * 0.5
        other = pltpu.roll(m, 64, 1)
        first = jnp.where(group % 2 == 0, m, other)
        second = jnp.where(group % 2 == 0, other, m)
        lanes = jnp.where(low, first, second)

        def mask(t):
            k = col * NK + t
            return lanes * jnp.where(low, mask_s[k].astype(F32), mask_s[k + TP].astype(F32))

        def pair(i):
            t = start + i * 2
            rhs = nb[p, pl.ds(t, 2)].reshape(256, CH)
            both = lax.dot_general(weights, rhs, (((1,), (1,)), ((), ())), preferred_element_type=F32)
            gated = (jnp.tanh(both[CH:]) + 1.0) * both[:CH]
            s32[pl.ds(t, CH, stride=TP), :] = gated[:, :128] * mask(t)
            s32[pl.ds(t + 1, CH, stride=TP), :] = gated[:, 128:] * mask(t + 1)

        loop(size // 2, pair, 4)

        def pack(i):
            if size == TP:
                rows = s32[pl.ds(pl.multiple_of(i * 4 * TP, 4 * TP), 4 * TP), :]
                send[p, pl.ds(i * 4, 4)] = rows.astype(BF16).reshape(4, TP, 128)
            else:
                for e in range(4):
                    rows = s32[pl.ds(pl.multiple_of((i * 4 + e) * TP + start, 16), size), :]
                    send[p, i * 4 + e, start : start + size] = rows.astype(BF16)

        loop(CH // 4, pack, 4)

    def gate(p):
        def body(i):
            t = i * 2
            v = nb[p, pl.ds(t, 2)].reshape(256, CH)
            g = jnp.dot(v, weights_in[4], preferred_element_type=F32)
            nb[p, pl.ds(t, 2)] = (0.5 * jnp.tanh(0.5 * g) + 0.5).astype(BF16).reshape(2, 128, CH)

        loop(TP // 2, body, 2)

    def two_rows(ref, p, y, q):
        a = ref[p, pl.ds((2 * y) * N_COL + q, 4)].astype(F32).reshape(4 * TP, 128)
        b = ref[p, pl.ds((2 * y + 1) * N_COL + q, 4)].astype(F32).reshape(4 * TP, 128)
        h0, h1 = swap_halves(a, b)
        both = jnp.concatenate([h0.reshape(4, 1, TP, 128), h1.reshape(4, 1, TP, 128)], axis=1)
        return both.reshape(4 * NK, 128).astype(BF16)

    def take_right(p):
        def body(i):
            y, q = i // 4, i % 4 * 4
            tile = two_rows(recv_r, p, y, q).T
            lane = pl.ds(pl.multiple_of(q * NK, 128), 4 * NK)
            for x in range(2):
                at = pl.multiple_of((2 * y + x) * NI + p * IP, IP)
                right_t[pl.ds(at, IP), lane] = tile[x * 64 : (x + 1) * 64]

        loop(16, body)

    def take_left(p):
        def body(i):
            y, q = i // 4, i % 4 * 4
            left[y, pl.ds(pl.multiple_of(q * NK, 128), 4 * NK), :] = two_rows(recv_l, p, y, q)

        loop(16, body)

    def product(s):
        def body(i):
            y, h = i // 4 * 2, i % 4
            rows = right_t[pl.ds(pl.multiple_of(h * 384, 384), 384), :]
            cols = jnp.concatenate([left[y], left[y + 1]], axis=1)
            tri = jnp.dot(rows, cols, preferred_element_type=F32)
            for x in range(2):
                both = tri[:, x * 128 : (x + 1) * 128].reshape(4, 2, TP, 128)
                e = swap_halves(both[:, 0].reshape(4 * TP, 128), both[:, 1].reshape(4 * TP, 128))
                for r in range(2):
                    slot = (2 * (y + x) + r) * N_COL + h * 4
                    send_r[s, pl.ds(slot, 4)] = e[r].astype(BF16).reshape(4, TP, 128)

        loop(8, body)

    def finish(s, start=0, size=TP):
        step = 16

        def norm(g):
            at = pl.multiple_of(start + g * 16, 16)
            rows = pl.ds(at, 16)

            def some(i):
                return recv_t[s, pl.ds(i * step, step), rows, :].astype(F32)

            zero = jnp.zeros((16, 128), F32)
            mean = lax.fori_loop(0, CH // step, lambda i, a: a + jnp.sum(some(i), axis=0), zero) * (1 / CH)

            def square(i, a):
                c = some(i) - mean[None]
                return a + jnp.sum(c * c, axis=0)

            var = lax.fori_loop(0, CH // step, square, zero) * (1 / CH)
            scale = lax.rsqrt(var + EPS)

            def put(i):
                c = some(i) - mean[None]
                for e in range(step):
                    ch = i * step + e
                    s32[pl.ds(pl.multiple_of(ch * TP + at, 16), 16), :] = c[e] * scale * og_s[ch] + ob_s[ch]

            loop(CH // step, put)

        loop(size // 16, norm)

        def tile(i):
            t = start + i
            v = s32[pl.ds(t, CH, stride=TP), :].astype(BF16)
            proj = jnp.dot(v.T, weights_in[5], preferred_element_type=F32)
            update = (proj * nb[s, t].astype(F32)).astype(BF16)
            out[t, s * IP : (s + 1) * IP] = update[:64]
            out[t + TP, s * IP : (s + 1) * IP] = update[64:]

        loop(size, tile, 16)

    load(0).wait()
    for start, size in ((0, 16), (16, 32)):
        normalise(0, start, size)
        project(0, 0, send_r, start, size)
        if start == 0:
            pl.semaphore_wait(barrier, N_DEV - 1)
        send_part(send_r, recv_r, 0, rs, rr, start, size, 4)
    for p in range(1, PARTS):
        load(p).wait()
        normalise(p)
        project(p, 0, send_r)
        send_part(send_r, recv_r, p, rs, rr)
    for p in range(PARTS):
        project(p, 1, send_l)
        send_part(send_l, recv_l, p, ls, lr)
    for p in range(PARTS):
        gate(p)
    for p in range(PARTS):
        wait_part(recv_r, p, rr)
        take_right(p)
    last = PARTS - 1
    for p in range(PARTS):
        wait_part(send_r, p, rs)
        wait_part(recv_l, p, lr)
        take_left(p)
        product(p)
        if p < last:
            send_part(send_r, recv_t, p, ts, tr)
        else:
            send_part(send_r, recv_t, p, ts, tr, 0, 32)
            send_part(send_r, recv_t, p, ts, tr2, 32, 16)
    for p in range(last):
        wait_part(recv_t, p, tr)
        finish(p)
    wait_part(recv_t, last, tr, 0, 32)
    finish(last, 0, 32)
    wait_part(recv_t, last, tr2, 32, 16)
    finish(last, 32, 16)
    for p in range(PARTS):
        wait_part(send_l, p, ls)
        wait_part(send_r, p, ts)


def on_device(
    pair_rep, res_mask, norm_gain, norm_bias, w_left, w_left_gate, w_right, w_right_gate, w_out_gate,
    out_gain, out_bias, w_out,
):
    vmem = pl.BlockSpec(memory_space=pltpu.VMEM)
    hbm = pl.BlockSpec(memory_space=pltpu.HBM)
    dma = pltpu.SemaphoreType.DMA
    slots = pltpu.VMEM((PARTS, N_DEV, TP, 128), BF16)
    return pl.pallas_call(
        kernel,
        out_shape=pltpu.VMEM((NK, NI, CH), BF16),
        in_specs=[hbm] * 13,
        out_specs=vmem,
        scratch_shapes=[
            pltpu.VMEM((PARTS, IP, NK, CH), BF16),
            pltpu.VMEM((PARTS, TP, 128, CH), BF16),
            pltpu.VMEM((IP * NK + NK, CH), F32),
            pltpu.VMEM((CH * TP + TP, 128), F32),
            pltpu.VMEM((4, CH, CH), BF16),
            slots, slots, slots, slots,
            pltpu.VMEM((N_COL * NK, N_COL * NK), BF16),
            pltpu.VMEM((4, N_COL * NK, 128), BF16),
            slots,
            pltpu.VMEM((12, 128), jnp.int32),
            pltpu.VMEM((1, CH), F32),
            pltpu.VMEM((1, CH), F32),
            pltpu.VMEM((6, CH, CH), BF16),
            pltpu.SMEM((N_COL * NK,), jnp.int32),
            pltpu.SMEM((CH,), F32),
            pltpu.SMEM((CH,), F32),
            dma((PARTS,)), dma((12,)),
            dma((PARTS,)), dma((PARTS,)), dma((PARTS,)), dma((PARTS,)), dma((PARTS,)), dma((PARTS,)), dma((PARTS,)),
        ],
        compiler_params=pltpu.CompilerParams(
            collective_id=0, has_side_effects=True, vmem_limit_bytes=58 << 20
        ),
        cost_estimate=pl.CostEstimate(flops=11 * 10**9, bytes_accessed=10**7, transcendentals=7 * 10**6),
    )(
        pair_rep, res_mask.reshape(12, 128), res_mask, norm_gain[None], norm_bias[None], w_right, w_right_gate, w_left,
        w_left_gate, w_out_gate, w_out, out_gain, out_bias,
    )


def solution(mesh):
    placed = (P("row", "col", None), P(), P(), P(), P(), P(), P(), P(), P(), P(), P(), P())
    return jax.shard_map(
        on_device, mesh=mesh, in_specs=placed, out_specs=P("col", "row", None), check_vma=False
    )
```
